32 devices in a mesh: dp: 16 (over z, y, core), tensor: 2 (over x).
Axes of the slice: x: 2, y: 2, z: 4, core: 2. Of those that a mesh axis runs over, the one named last changes fastest.
Arguments:
- tokens: bfloat16 [16, 1024, 768], P('dp', 'tensor'), may hold values from -6 to 6
- cotangent: bfloat16 [16, 1024, 768], P('dp', 'tensor'), may hold values from -6 to 6
- norm_in: float32 [768], replicated, may hold values from 0.5 to 1.5
- gate_inner_projection: bfloat16 [768, 2, 1536], P('dp', None, 'tensor'), may hold values from -0.21875 to 0.21875
- proj_bc: bfloat16 [768, 256], P('dp'), may hold values from -0.21875 to 0.21875
- proj_dt: bfloat16 [768, 24], P('dp', 'tensor'), may hold values from -0.21875 to 0.21875
- conv_inner: float32 [4, 1536], P(None, 'tensor'), may hold values from -3 to 3
- bias_inner: float32 [1536], P('tensor'), may hold values from -0.5 to 0.5
- conv_bc: float32 [4, 256], replicated, may hold values from -3 to 3
- bias_bc: float32 [256], replicated, may hold values from -0.5 to 0.5
- step_bias: float32 [24], P('tensor'), may hold values from -7 to -2
- log_decay: float32 [24], P('tensor'), may hold values from -1.5 to 2.5
- skip_gain: float32 [24], P('tensor'), may hold values from 0.5 to 2
- norm_gate: float32 [1536], P('tensor'), may hold values from 0.5 to 1.5
- proj_out: bfloat16 [1536, 768], P('tensor', 'dp'), may hold values from -0.15625 to 0.15625
Outputs:
- block_out: bfloat16 [16, 1024, 768], P('dp', 'tensor')
- input_grad: float32 [16, 1024, 768], P('dp', 'tensor')
- grad_norm_in: float32 [768], replicated
- grad_proj_zx: float32 [768, 2, 1536], P('dp', None, 'tensor')
- grad_proj_bc: float32 [768, 256], P('dp')
- grad_proj_dt: float32 [768, 24], P('dp', 'tensor')
- grad_conv_inner: float32 [4, 1536], P(None, 'tensor')
- grad_bias_inner: float32 [1536], P('tensor')
- grad_conv_bc: float32 [4, 256], replicated
- grad_bias_bc: float32 [256], replicated
- grad_step_bias: float32 [24], P('tensor')
- grad_log_decay: float32 [24], P('tensor')
- grad_skip_gain: float32 [24], P('tensor')
- grad_norm_gate: float32 [1536], P('tensor')
- grad_proj_out: float32 [1536, 768], P('tensor', 'dp')
The draws below stay inside these ranges and needn't reach their ends.
All inputs are finite; a program needn't handle non-finite values.
Results may differ from the reference program's by a relative error of at most 0.018.
Values may be sent and summed in bfloat16 or wider, within the bound.
A program may use at most 128 MiB of HBM per device.

```python
import math
import jax
import jax.numpy as jnp
from jax import lax

D = 768
HEADS = 24
NSTATE = 128
CONV = 4
SPAN = 256
INNER = 1536
LEN = 1024
SEQS = 16


def level_of(key, dims, pieces, least, top_value):
    def one(axis_at, blocks):
        heights = jax.random.uniform(jax.random.fold_in(jax.random.fold_in(key, 6), axis_at), (blocks,), jnp.float32, least / len(pieces), top_value / len(pieces))
        return jnp.repeat(jnp.exp(heights), dims[axis_at] // blocks).reshape((-1,) + (1,) * (len(dims) - axis_at - 1))

    level = one(*pieces[0])
    for cut in pieces[1:]:
        level = level * one(*cut)
    return level


def scatter_about(stream_key, shape, spread, reach, split=(), held_as=jnp.bfloat16):
    values = spread * jax.random.normal(stream_key, shape, jnp.float32)
    if split:
        values = values * level_of(stream_key, shape, split, -0.22, 0.18)
    return jnp.clip(values, -reach, reach).astype(held_as)


def setup_inputs(seed: int = 0) -> dict:
    splits = jax.random.split(jax.random.key(seed), 16)
    tokens = scatter_about(splits[0], (SEQS, LEN, D), 1.0, 6.0, ((0, 16), (1, 2)))
    cotangent = scatter_about(splits[1], (SEQS, LEN, D), 1.0, 6.0, ((0, 16), (1, 2)))
    norm_in = jnp.clip(1.0 + 0.1 * jax.random.normal(splits[2], (D,), jnp.float32), 0.5, 1.5)
    gate_inner_projection = scatter_about(splits[3], (D, 2, INNER), D ** -0.5, 0.21875, ((0, 16), (2, 2)))
    proj_bc = scatter_about(splits[4], (D, 2 * NSTATE), D ** -0.5, 0.21875, ((0, 16),))
    proj_dt = scatter_about(splits[5], (D, HEADS), D ** -0.5, 0.21875, ((0, 16), (1, 2)))
    conv_inner = scatter_about(splits[6], (CONV, INNER), CONV ** -0.5, 3.0, ((1, 2),), jnp.float32)
    bias_inner = jnp.clip(jax.random.uniform(splits[7], (INNER,), jnp.float32, -0.5, 0.5) * level_of(splits[7], (INNER,), ((0, 2),), -0.4, 0.0), -0.5, 0.5)
    conv_bc = scatter_about(splits[8], (CONV, 2 * NSTATE), CONV ** -0.5, 3.0, (), jnp.float32)
    bias_bc = jnp.clip(jax.random.uniform(splits[9], (2 * NSTATE,), jnp.float32, -0.5, 0.5), -0.5, 0.5)
    step_bias = jnp.clip(-7.0 + 5.0 * jax.random.uniform(splits[10], (HEADS,), jnp.float32) ** level_of(splits[10], (HEADS,), ((0, 2),), -0.2, 0.2), -7.0, -2.0)
    log_decay = jnp.clip(-1.5 + 4.0 * jax.random.uniform(splits[11], (HEADS,), jnp.float32) ** level_of(splits[11], (HEADS,), ((0, 2),), -0.2, 0.2), -1.5, 2.5)
    skip_gain = jnp.clip(0.5 + 1.5 * jax.random.uniform(splits[12], (HEADS,), jnp.float32) ** level_of(splits[12], (HEADS,), ((0, 2),), -0.2, 0.2), 0.5, 2.0)
    norm_gate = jnp.clip(1.0 + 0.1 * jax.random.normal(splits[13], (INNER,), jnp.float32), 0.5, 1.5)
    proj_out = scatter_about(splits[14], (INNER, D), INNER ** -0.5, 0.15625, ((0, 2), (1, 16)))
    return dict(tokens=tokens, cotangent=cotangent, norm_in=norm_in, gate_inner_projection=gate_inner_projection, proj_bc=proj_bc, proj_dt=proj_dt, conv_inner=conv_inner, bias_inner=bias_inner, conv_bc=conv_bc, bias_bc=bias_bc, step_bias=step_bias, log_decay=log_decay, skip_gain=skip_gain, norm_gate=norm_gate, proj_out=proj_out)


EPSILON = 1e-05
TOP_PRECISION = lax.Precision.HIGHEST

@jax.custom_vjp
def low(v):
    return lax.optimization_barrier(v.astype(jnp.bfloat16)).astype(jnp.float32)

@jax.custom_vjp
def reduced_precision_back(v):
    return v

def low_keep(v):
    return (low(v), None)

def low_pass(kept, grad):
    return (grad,)

def back_keep(v):
    return (v, None)

def back_low(kept, grad):
    return (low(grad),)
low.defvjp(low_keep, low_pass)
reduced_precision_back.defvjp(back_keep, back_low)

def scan_block(carry_state, block_data):
    scaled_in, key_matrix, query_matrix, decay_factor = block_data
    size_q = decay_factor.shape[0]
    cumulative = jnp.cumsum(decay_factor, axis=0)
    row_index = lax.broadcasted_iota(jnp.int32, (size_q, size_q), 0)
    col_index = lax.broadcasted_iota(jnp.int32, (size_q, size_q), 1)
    causal = (col_index <= row_index)[None]
    log_gap = cumulative.T[:, :, None] - cumulative.T[:, None, :]
    decay_table = jnp.exp(jnp.where(causal, log_gap, -jnp.inf))
    scores = jnp.dot(query_matrix, key_matrix.T, precision=TOP_PRECISION)
    weights = decay_table * scores[None]
    intra_out = jnp.einsum('hij,jhp->ihp', weights, scaled_in, precision=TOP_PRECISION)
    inter_out = jnp.einsum('in,hpn->ihp', query_matrix, carry_state, precision=TOP_PRECISION) * jnp.exp(cumulative)[:, :, None]
    tail_decay = jnp.exp(cumulative[-1][None, :] - cumulative)
    fresh_state = jnp.einsum('jhp,jn->hpn', scaled_in * tail_decay[:, :, None], key_matrix, precision=TOP_PRECISION)
    carry_state = jnp.exp(cumulative[-1])[:, None, None] * carry_state + fresh_state
    return (carry_state, intra_out + inter_out)

def scan_heads(scaled_in, key_matrix, query_matrix, decay_factor):
    length, head_count, head_width = scaled_in.shape
    block_count = length // SPAN
    blocks = (scaled_in.reshape(block_count, SPAN, head_count, head_width), key_matrix.reshape(block_count, SPAN, key_matrix.shape[1]), query_matrix.reshape(block_count, SPAN, query_matrix.shape[1]), decay_factor.reshape(block_count, SPAN, head_count))
    start_state = jnp.zeros((head_count, head_width, key_matrix.shape[1]), jnp.float32)
    final_state, outputs = lax.scan(jax.checkpoint(scan_block), start_state, blocks)
    return outputs.reshape(length, head_count, head_width)

def causal_conv(values, kernel, offset):
    tap_count = kernel.shape[0]
    length = values.shape[0]
    padded_tokens = jnp.pad(values, ((tap_count - 1, 0), (0, 0)))
    summed = jnp.zeros_like(values) + offset[None, :]
    for position in range(tap_count):
        summed = summed + kernel[position][None, :] * padded_tokens[position:position + length]
    return summed

def mixer(inner_act, state_mats, step_raw, step_bias, log_decay, skip_gain):
    length = inner_act.shape[0]
    head_count = step_raw.shape[1]
    step_size = jax.nn.softplus(step_raw + step_bias)
    decay_factor = -jnp.exp(log_decay) * step_size
    per_head = inner_act.reshape(length, head_count, -1)
    scaled_in = per_head * step_size[:, :, None]
    scanned = scan_heads(scaled_in, state_mats[:, :NSTATE], state_mats[:, NSTATE:], decay_factor)
    return (scanned + skip_gain[None, :, None] * per_head).reshape(length, -1)

def layer_forward(sequences, norm_in, gate_inner_projection, proj_bc, proj_dt, conv_inner, bias_inner, conv_bc, bias_bc, step_bias, log_decay, skip_gain, norm_gate, proj_out):
    inv_rms = lax.rsqrt(lax.optimization_barrier(jnp.mean(sequences * sequences, axis=-1, keepdims=True)) + EPSILON)
    normalized_rows = low(sequences * inv_rms * norm_in)
    inner_gate_values = reduced_precision_back(jnp.einsum('kup,pwm->kuwm', normalized_rows, gate_inner_projection, precision=TOP_PRECISION))
    state_raw = reduced_precision_back(jnp.einsum('bld,dn->bln', normalized_rows, proj_bc, precision=TOP_PRECISION))
    step_raw = reduced_precision_back(jnp.einsum('bld,dh->blh', normalized_rows, proj_dt, precision=TOP_PRECISION))
    convolve = jax.vmap(causal_conv, in_axes=(0, None, None))
    inner_act = low(jax.nn.silu(convolve(inner_gate_values[:, :, 1], conv_inner, bias_inner)))
    state_mats = low(jax.nn.silu(convolve(state_raw, conv_bc, bias_bc)))
    scanned = jax.vmap(mixer, in_axes=(0, 0, 0, None, None, None))(inner_act, state_mats, step_raw, step_bias, log_decay, skip_gain)
    gated = scanned * jax.nn.silu(inner_gate_values[:, :, 0])
    gate_scale = lax.rsqrt(lax.optimization_barrier(jnp.mean(gated * gated, axis=-1, keepdims=True)) + EPSILON)
    gate_normed = low(gated * gate_scale * norm_gate)
    return sequences + jnp.einsum('bli,id->bld', gate_normed, proj_out, precision=TOP_PRECISION)

def reference(tokens, cotangent, norm_in, gate_inner_projection, proj_bc, proj_dt, conv_inner, bias_inner, conv_bc, bias_bc, step_bias, log_decay, skip_gain, norm_gate, proj_out):
    params = (norm_in, gate_inner_projection, proj_bc, proj_dt, conv_inner, bias_inner, conv_bc, bias_bc, step_bias, log_decay, skip_gain, norm_gate, proj_out)
    params = tuple((value.astype(jnp.float32) for value in params))
    group = math.gcd(SEQS, max(1, 4096 // LEN))
    batches = SEQS // group
    inputs = tokens.astype(jnp.float32).reshape(batches, group, LEN, D)
    cot_blocks = cotangent.astype(jnp.float32).reshape(batches, group, LEN, D)

    def one_batch(totals, batch):
        block_in, cot_block = batch
        result, pull = jax.vjp(layer_forward, block_in, *params)
        grads = pull(cot_block)
        summed = tuple((left + right for left, right in zip(totals, grads[1:])))
        return (summed, (result.astype(jnp.bfloat16), grads[0]))
    zeros = tuple((jnp.zeros_like(value) for value in params))
    totals, (outputs, in_grads) = lax.scan(one_batch, zeros, (inputs, cot_blocks))
    return (outputs.reshape(SEQS, LEN, D), in_grads.reshape(SEQS, LEN, D), totals[0], totals[1], totals[2], totals[3], totals[4], totals[5], totals[6], totals[7], totals[8], totals[9], totals[10], totals[11], totals[12])
```

```python
import functools

import jax
import jax.numpy as jnp
from jax import lax
from jax.experimental import pallas as pl
from jax.experimental.pallas import tpu as pltpu
from jax.sharding import PartitionSpec as P

NSTATE = 128
SPAN = 256
INNER = 1536
PAD = 128
EPSILON = 1e-05
F32 = jnp.float32
BF16 = jnp.bfloat16
VMEM_LIMIT = 60 * 1024 * 1024


def mm(left, right, left_dim=1, right_dim=0):
    return lax.dot_general(
        left, right, (((left_dim,), (right_dim,)), ((), ())), preferred_element_type=F32
    )


def exact_mm(left, right):
    return lax.dot_general(
        left, right, (((1,), (0,)), ((), ())), preferred_element_type=F32,
        precision=lax.Precision.HIGHEST,
    )


def sigmoid(v):
    return 1.0 / (1.0 + jnp.exp(-v))


def iotas(size):
    return (
        lax.broadcasted_iota(jnp.int32, (size, size), 0),
        lax.broadcasted_iota(jnp.int32, (size, size), 1),
    )


def by_pair(values, pair, first_lanes):
    left = values[:, 2 * pair : 2 * pair + 1]
    right = values[:, 2 * pair + 1 : 2 * pair + 2]
    return jnp.where(first_lanes, left, right)


def steps_of(step_raw, hp):
    shifted = step_raw + hp[0:1, :]
    step = jnp.maximum(shifted, 0.0) + jnp.log1p(jnp.exp(-jnp.abs(shifted)))
    return shifted, step, -jnp.exp(hp[1:2, :]) * step


def forward_kernel(
    normed_ref, cot_ref, wcat_ref, out_ref, cw_ref, hp_ref, ch_ref,
    raw_ref, conv_ref, scanned_ref, gated_ref, state_out_ref, dng_ref, stats_ref,
    buf, state, fresh_in,
):
    at = pl.program_id(0)
    span = normed_ref.shape[0]
    width = scanned_ref.shape[1]
    both = width + 2 * NSTATE

    @pl.when(at == 0)
    def _():
        buf[0:8, :] = jnp.zeros((8, both), F32)
        state[...] = jnp.zeros_like(state)

    @pl.when(at > 0)
    def _():
        buf[0:8, :] = buf[span : span + 8, :]

    raw_ref[...] = mm(normed_ref[...], wcat_ref[...])
    buf[8 : 8 + span, :] = raw_ref[:, width : width + both]
    conv = cw_ref[4:5, :] + cw_ref[0:1, :] * buf[5 : 5 + span, :]
    for tap in range(1, 4):
        conv = conv + cw_ref[tap : tap + 1, :] * buf[5 + tap : 5 + tap + span, :]
    conv_ref[...] = conv
    act = (conv * sigmoid(conv)).astype(BF16)
    km = act[:, width : width + NSTATE]
    qm = act[:, width + NSTATE :]
    shifted, step, rate = steps_of(raw_ref[:, width + both :], hp_ref[...])
    rows, cols = iotas(span)
    causal = cols <= rows
    cum = exact_mm(jnp.where(causal, 1.0, 0.0), rate)
    cum_t = cum.T
    grow = jnp.exp(cum)
    last = cum[span - 1 : span, :]
    tail = jnp.exp(last - cum)
    total = jnp.exp(last)
    scores = jnp.where(causal, mm(qm, km, 1, 1), 0.0)
    state_now = state[...]
    state_out_ref[...] = state_now
    inter = mm(qm, state_now.astype(BF16))
    first = lax.broadcasted_iota(jnp.int32, (span, 128), 1) < 64
    for pair in range(width // 128):
        lanes = slice(pair * 128, pair * 128 + 128)
        x = act[:, lanes].astype(F32)
        u = x * by_pair(step, pair, first)
        fresh_in[:, lanes] = (u * by_pair(tail, pair, first)).astype(BF16)
        low_u = u.astype(BF16)
        ys = []
        for head in (2 * pair, 2 * pair + 1):
            gap = jnp.minimum(cum[:, head : head + 1] - cum_t[head : head + 1, :], 0.0)
            ys.append(mm((jnp.exp(gap) * scores).astype(BF16), low_u))
        y = jnp.where(first, ys[0], ys[1]) + inter[:, lanes] * by_pair(grow, pair, first)
        scanned_ref[:, lanes] = y + ch_ref[0:1, lanes] * x
    fresh = mm(km, fresh_in[...], 0, 0)
    for pair in range(width // 128):
        lanes = slice(pair * 128, pair * 128 + 128)
        state[:, lanes] = (
            by_pair(total, pair, first[0:1]) * state_now[:, lanes] + fresh[:, lanes]
        )
    gate_z = raw_ref[:, 0:width]
    gated = scanned_ref[...] * (gate_z * sigmoid(gate_z))
    gated_ref[...] = gated
    dng = mm(cot_ref[...], out_ref[...])
    dng_ref[...] = dng
    squares = jnp.sum(gated * gated, axis=1, keepdims=True)
    cross = jnp.sum(dng * ch_ref[1:2, :] * gated, axis=1, keepdims=True)
    lane = lax.broadcasted_iota(jnp.int32, (span, PAD), 1)
    stats_ref[...] = jnp.where(lane == 0, squares, jnp.where(lane == 1, cross, 0.0))


def backward_kernel(
    normed_ref, raw_ref, conv_ref, scanned_ref, state_ref, dng_ref, stats_ref,
    wcat_ref, cw_ref, hp_ref, ch_ref, sum_ref,
    partial_ref, grads_ref, gcw_ref, ghp_ref, gch_ref,
    adjoint, buf, acc, dye, ut, dz, prod, score_sum,
):
    at = pl.program_id(0)
    span = normed_ref.shape[0]
    width = scanned_ref.shape[1]
    both = width + 2 * NSTATE

    @pl.when(at == 0)
    def _():
        buf[span : span + 8, :] = jnp.zeros((8, both), F32)
        adjoint[...] = jnp.zeros_like(adjoint)
        acc[...] = jnp.zeros_like(acc)
        gcw_ref[...] = jnp.zeros_like(gcw_ref)
        ghp_ref[...] = jnp.zeros_like(ghp_ref)
        gch_ref[...] = jnp.zeros_like(gch_ref)

    @pl.when(at > 0)
    def _():
        buf[span : span + 8, :] = buf[0:8, :]

    stats = stats_ref[...]
    scale = lax.rsqrt(stats[:, 0:1] / INNER + EPSILON)
    pull = scale * scale * scale * stats[:, 1:2] / INNER
    gate_z = raw_ref[:, 0:width]
    sig = sigmoid(gate_z)
    silu = gate_z * sig
    scanned = scanned_ref[...]
    gated = scanned * silu
    dng = dng_ref[...]
    d_gated = scale * (dng * ch_ref[1:2, :]) - gated * pull
    gch_ref[1:2, :] += jnp.sum(dng * gated * scale, axis=0, keepdims=True)
    dy = d_gated * silu
    dz[:, 0:width] = (d_gated * scanned * (sig * (1.0 + gate_z * (1.0 - sig)))).astype(BF16)

    conv = conv_ref[...]
    sig_conv = sigmoid(conv)
    act = (conv * sig_conv).astype(BF16)
    slope = sig_conv * (1.0 + conv * (1.0 - sig_conv))
    km = act[:, width : width + NSTATE]
    qm = act[:, width + NSTATE :]
    hp = hp_ref[...]
    shifted, step, rate = steps_of(raw_ref[:, width + both :], hp)
    rows, cols = iotas(span)
    causal = cols <= rows
    cum = exact_mm(jnp.where(causal, 1.0, 0.0), rate)
    cum_t = cum.T
    grow = jnp.exp(cum)
    last = cum[span - 1 : span, :]
    tail = jnp.exp(last - cum)
    total = jnp.exp(last)
    scores = mm(qm, km, 1, 1)
    state = state_ref[...]
    low_state = state.astype(BF16)
    adj = adjoint[...]
    low_adj = adj.astype(BF16)
    inter = mm(qm, low_state)
    du_state = mm(km, low_adj)
    first = lax.broadcasted_iota(jnp.int32, (span, 128), 1) < 64
    lane = lax.broadcasted_iota(jnp.int32, (span, PAD), 1)
    row_sums = jnp.zeros((span, PAD), F32)
    col_sums = []
    for pair in range(width // 128):
        lanes = slice(pair * 128, pair * 128 + 128)
        x = act[:, lanes].astype(F32)
        step_pair = by_pair(step, pair, first)
        tail_pair = by_pair(tail, pair, first)
        u = x * step_pair
        low_u = u.astype(BF16)
        u_tail = u * tail_pair
        ut[:, lanes] = u_tail.astype(BF16)
        dy_pair = dy[:, lanes]
        low_dy = dy_pair.astype(BF16)
        dy_grow = dy_pair * by_pair(grow, pair, first)
        dye[:, lanes] = dy_grow.astype(BF16)
        prod[0:span, lanes] = dy_grow * inter[:, lanes]
        prod[span : 2 * span, lanes] = u_tail * du_state[:, lanes]
        dus = []
        for head in (2 * pair, 2 * pair + 1):
            mine = first if head % 2 == 0 else jnp.logical_not(first)
            d_weights = mm(jnp.where(mine, low_dy, jnp.zeros_like(low_dy)), low_u, 1, 1)
            gap = cum[:, head : head + 1] - cum_t[head : head + 1, :]
            table = jnp.exp(jnp.where(causal, gap, -1e30))
            weights = table * scores
            d_scores = table * d_weights
            if head == 0:
                score_sum[...] = d_scores
            else:
                score_sum[...] += d_scores
            moved = weights * d_weights
            row_sums = jnp.where(
                lane == head, jnp.sum(moved, axis=1, keepdims=True), row_sums
            )
            col_sums.append(jnp.sum(moved, axis=0, keepdims=True))
            dus.append(mm(weights.astype(BF16), low_dy, 0, 0))
        du = jnp.where(first, dus[0], dus[1]) + du_state[:, lanes] * tail_pair
        prod[2 * span : 3 * span, lanes] = x * du
        gch_ref[0:1, lanes] += jnp.sum(dy_pair * x, axis=0, keepdims=True)
        dx = step_pair * du + ch_ref[0:1, lanes] * dy_pair
        buf[0:span, lanes] = dx * slope[:, lanes]
    col_sums.append(jnp.zeros((PAD - len(col_sums), span), F32))
    col_sums = jnp.concatenate(col_sums, axis=0).T
    prods = prod[...]
    high = prods.astype(BF16)
    low = (prods - high.astype(F32)).astype(BF16)
    summer = sum_ref[...]
    heads = mm(high, summer) + mm(low, summer)
    met = jnp.sum(adj * state, axis=0, keepdims=True)
    met = jnp.broadcast_to(met, (8, width))
    met_high = met.astype(BF16)
    met_low = (met - met_high.astype(F32)).astype(BF16)
    met = (mm(met_high, summer) + mm(met_low, summer))[0:1, :]
    d_rate = (
        exact_mm(jnp.where(cols >= rows, 1.0, 0.0), row_sums - col_sums + heads[0:span])
        + exact_mm(jnp.where(cols < rows, 1.0, 0.0), heads[span : 2 * span])
        + total * met
    )
    d_step = heads[2 * span :] - jnp.exp(hp[1:2, :]) * d_rate
    d_step_raw = d_step * sigmoid(shifted)
    ghp_ref[0:1, :] += jnp.sum(d_step_raw, axis=0, keepdims=True)
    ghp_ref[1:2, :] += jnp.sum(d_rate * rate, axis=0, keepdims=True)
    dz[:, width + both :] = d_step_raw.astype(BF16)

    low_sum = score_sum[...].astype(BF16)
    dk = mm(low_sum, qm, 0, 0) + mm(ut[...], low_adj, 1, 1)
    dq = mm(low_sum, km) + mm(dye[...], low_state, 1, 1)
    buf[0:span, width : width + NSTATE] = dk * slope[:, width : width + NSTATE]
    buf[0:span, width + NSTATE : both] = dq * slope[:, width + NSTATE :]
    raw = raw_ref[:, width : width + both]
    gcw_ref[4:5, :] += jnp.sum(buf[0:span, :], axis=0, keepdims=True)
    d_raw = jnp.zeros((span, both), F32)
    for tap in range(4):
        moved = buf[3 - tap : 3 - tap + span, :]
        d_raw = d_raw + cw_ref[tap : tap + 1, :] * moved
        gcw_ref[tap : tap + 1, :] += jnp.sum(raw * moved, axis=0, keepdims=True)
    dz[:, width : width + both] = d_raw.astype(BF16)

    low_dz = dz[...]
    partial_ref[...] = mm(low_dz, wcat_ref[...], 1, 1).astype(BF16)
    acc[...] += mm(normed_ref[...], low_dz, 0, 0)
    fresh = mm(qm, dye[...], 0, 0)
    for pair in range(width // 128):
        lanes = slice(pair * 128, pair * 128 + 128)
        adjoint[:, lanes] = by_pair(total, pair, first[0:1]) * adj[:, lanes] + fresh[:, lanes]

    @pl.when(at == pl.num_programs(0) - 1)
    def _():
        grads_ref[...] = acc[...].astype(BF16)


def forward_part(normed, cot, wcat, out_t, cw, hp, ch):
    length, model = normed.shape
    width = ch.shape[1]
    both = width + 2 * NSTATE
    cat = wcat.shape[1]
    blocks = length // SPAN
    row = lambda cols: pl.BlockSpec((SPAN, cols), lambda i: (i, 0))
    whole = lambda arr: pl.BlockSpec(arr.shape, lambda i: (0, 0))
    shape = lambda r, c: jax.ShapeDtypeStruct((r, c), F32)
    return pl.pallas_call(
        forward_kernel,
        grid=(blocks,),
        in_specs=[row(model), row(model), whole(wcat), whole(out_t), whole(cw), whole(hp), whole(ch)],
        out_specs=[
            row(cat), row(both), row(width), row(width),
            pl.BlockSpec((NSTATE, width), lambda i: (i, 0)), row(width), row(PAD),
        ],
        out_shape=[
            shape(length, cat), shape(length, both), shape(length, width), shape(length, width),
            shape(blocks * NSTATE, width), shape(length, width), shape(length, PAD),
        ],
        scratch_shapes=[
            pltpu.VMEM((SPAN + 8, both), F32),
            pltpu.VMEM((NSTATE, width), F32),
            pltpu.VMEM((SPAN, width), BF16),
        ],
        compiler_params=pltpu.CompilerParams(vmem_limit_bytes=VMEM_LIMIT),
        cost_estimate=pl.CostEstimate(
            flops=2 * length * (model * (cat + width) + 4 * SPAN * width),
            bytes_accessed=25 * 2**20, transcendentals=length * width * 6,
        ),
        name="mixer_forward",
    )(normed, cot, wcat, out_t, cw, hp, ch)


def backward_part(normed, raw, conv, scanned, states, dng, stats, wcat, cw, hp, ch):
    length, model = normed.shape
    width = ch.shape[1]
    both = width + 2 * NSTATE
    cat = wcat.shape[1]
    blocks = length // SPAN
    summer = (
        lax.broadcasted_iota(jnp.int32, (width, PAD), 0) // 64
        == lax.broadcasted_iota(jnp.int32, (width, PAD), 1)
    ).astype(BF16)
    row = lambda cols: pl.BlockSpec((SPAN, cols), lambda i: (blocks - 1 - i, 0))
    whole = lambda arr: pl.BlockSpec(arr.shape, lambda i: (0, 0))
    return pl.pallas_call(
        backward_kernel,
        grid=(blocks,),
        in_specs=[
            row(model), row(cat), row(both), row(width),
            pl.BlockSpec((NSTATE, width), lambda i: (blocks - 1 - i, 0)), row(width), row(PAD),
            whole(wcat), whole(cw), whole(hp), whole(ch), whole(summer),
        ],
        out_specs=[row(model), whole(wcat), whole(cw), whole(hp), whole(ch)],
        out_shape=[
            jax.ShapeDtypeStruct((length, model), BF16),
            jax.ShapeDtypeStruct((model, cat), BF16),
            jax.ShapeDtypeStruct(cw.shape, F32),
            jax.ShapeDtypeStruct(hp.shape, F32),
            jax.ShapeDtypeStruct(ch.shape, F32),
        ],
        scratch_shapes=[
            pltpu.VMEM((NSTATE, width), F32),
            pltpu.VMEM((SPAN + 8, both), F32),
            pltpu.VMEM((model, cat), F32),
            pltpu.VMEM((SPAN, width), BF16),
            pltpu.VMEM((SPAN, width), BF16),
            pltpu.VMEM((SPAN, cat), BF16),
            pltpu.VMEM((3 * SPAN, width), F32),
            pltpu.VMEM((SPAN, SPAN), F32),
        ],
        compiler_params=pltpu.CompilerParams(vmem_limit_bytes=VMEM_LIMIT),
        cost_estimate=pl.CostEstimate(
            flops=2 * length * (2 * model * cat + 10 * SPAN * width),
            bytes_accessed=25 * 2**20, transcendentals=length * width * 8,
        ),
        name="mixer_adjoint",
    )(normed, raw, conv, scanned, states, dng, stats, wcat, cw, hp, ch, summer)


def swap(values, bit, axis, size):
    return lax.ppermute(values, axis, [(i, i ^ bit) for i in range(size)])


def scatter_sum(values, size, order):
    me = lax.axis_index("dp")
    bits = size.bit_length() - 1
    rows = values.shape[0] // size
    held = values.reshape((2,) * bits + (rows, values.shape[1]))
    left = list(range(bits - 1, -1, -1))
    for bit in order:
        axis = left.index(bit)
        mine = (me >> bit) & 1
        keep = lax.dynamic_index_in_dim(held, mine, axis, keepdims=False)
        send = lax.dynamic_index_in_dim(held, 1 - mine, axis, keepdims=False)
        got = swap(send, 1 << bit, "dp", size)
        held = (keep.astype(F32) + got.astype(F32)).astype(BF16)
        left.pop(axis)
    return held


def whole_sum(values, axis, size):
    bit = 1
    while bit < size:
        values = values + swap(values, bit, axis, size)
        bit *= 2
    return values


def token_scatter(values, size):
    if size != 2:
        return lax.psum_scatter(values, "tensor", scatter_dimension=0, tiled=True).astype(F32)
    me = lax.axis_index("tensor")
    half = values.shape[0] // 2
    keep = lax.dynamic_slice_in_dim(values, me * half, half, 0)
    send = lax.dynamic_slice_in_dim(values, (1 - me) * half, half, 0)
    return keep.astype(F32) + swap(send, 1, "tensor", 2).astype(F32)


def on_device(
    dp, tp,
    tokens, cotangent, norm_in, gate_inner_projection, proj_bc, proj_dt, conv_inner,
    bias_inner, conv_bc, bias_bc, step_bias, log_decay, skip_gain, norm_gate, proj_out,
):
    width = gate_inner_projection.shape[2]
    heads = step_bias.shape[0]
    model = tokens.shape[2]
    share = model // dp
    cat = 2 * width + 2 * NSTATE + PAD
    packed = jnp.concatenate(
        [
            gate_inner_projection.reshape(share, 2 * width),
            proj_bc,
            jnp.pad(proj_dt, ((0, 0), (0, PAD - heads))),
            proj_out.T,
        ],
        axis=1,
    )
    weights = lax.all_gather(packed, "dp", axis=0, tiled=True)
    wcat, out_t = weights[:, :cat], weights[:, cat:]
    token_rows = tokens[0].astype(F32)
    inv_rms = lax.rsqrt(jnp.mean(token_rows * token_rows, axis=-1, keepdims=True) + EPSILON)
    local_normed = (token_rows * inv_rms * norm_in).astype(BF16)
    normed = lax.all_gather(local_normed, "tensor", axis=0, tiled=True)
    cot = lax.all_gather(cotangent[0], "tensor", axis=0, tiled=True)
    cw = jnp.pad(
        jnp.concatenate(
            [
                jnp.concatenate([conv_inner, conv_bc], axis=1),
                jnp.concatenate([bias_inner, bias_bc])[None],
            ],
            axis=0,
        ),
        ((0, 3), (0, 0)),
    )
    hp = jnp.pad(jnp.stack([step_bias, log_decay]), ((0, 6), (0, PAD - heads)))
    ch = jnp.pad(jnp.stack([jnp.repeat(skip_gain, width // heads), norm_gate]), ((0, 6), (0, 0)))
    raw, conv, scanned, gated, states, dng, stats = forward_part(
        normed, cot, wcat, out_t, cw, hp, ch
    )
    stats = jnp.pad(
        whole_sum(stats[:, :2].T, "tensor", tp).T, ((0, 0), (0, PAD - 2))
    )
    scale = lax.rsqrt(stats[:, 0:1] / INNER + EPSILON)
    gate_normed = (gated * scale * norm_gate).astype(BF16)
    branch = token_scatter(mm(gate_normed, out_t, 1, 1).astype(BF16), tp)
    block_out = (token_rows + branch).astype(BF16)[None]
    bits = dp.bit_length() - 1
    order = tuple(range(bits))
    other = (0,) + tuple(range(2, bits)) + (1,)
    grad_out = scatter_sum(mm(cot, gate_normed, 0, 0).astype(BF16), dp, other)
    partial, grads, gcw, ghp, gch = backward_part(
        normed, raw, conv, scanned, states, dng, stats, wcat, cw, hp, ch
    )
    cut = cat // 256 * 128
    grads = jnp.concatenate(
        [scatter_sum(grads[:, :cut], dp, order), scatter_sum(grads[:, cut:], dp, other)], axis=1
    )
    d_rows = token_scatter(partial, tp)
    gained = norm_in * d_rows
    dotted = jnp.sum(token_rows * gained, axis=-1, keepdims=True)
    input_grad = (
        cotangent[0].astype(F32)
        + inv_rms * gained
        - token_rows * (inv_rms * inv_rms * inv_rms * dotted / model)
    )[None]
    grad_norm_in = jnp.sum(d_rows * token_rows * inv_rms, axis=0)
    grad_skip = jnp.sum(gch[0].reshape(heads, -1), axis=1)
    mine = [gcw[:5, :width].reshape(-1), ghp[0, :heads], ghp[1, :heads], grad_skip, gch[1]]
    common = [gcw[:5, width:].reshape(-1), grad_norm_in]
    sizes = [v.shape[0] for v in mine + common]
    flat = jnp.concatenate(mine + common)
    count = flat.shape[0]
    flat = jnp.pad(flat, (0, -count % 1024)).reshape(-1, 128)
    flat = whole_sum(flat, "dp", dp).reshape(-1)[:count]
    own = sum(sizes[: len(mine)])
    grad_bc = grads[:, 2 * width : 2 * width + 2 * NSTATE].astype(F32)
    shared = jnp.concatenate([grad_bc.reshape(-1), flat[own:]])
    shared = whole_sum(shared.reshape(-1, 128), "tensor", tp).reshape(-1)
    grad_bc = shared[: grad_bc.size].reshape(grad_bc.shape)
    shared = shared[grad_bc.size :]
    parts = jnp.split(flat[:own], [sum(sizes[:i]) for i in range(1, len(mine))])
    gconv = parts[0].reshape(5, width)
    gbc = shared[: sizes[len(mine)]].reshape(5, 2 * NSTATE)
    return (
        block_out,
        input_grad,
        shared[sizes[len(mine)] :],
        grads[:, : 2 * width].astype(F32).reshape(share, 2, width),
        grad_bc,
        grads[:, 2 * width + 2 * NSTATE :][:, :heads].astype(F32),
        gconv[:4],
        gconv[4],
        gbc[:4],
        gbc[4],
        parts[1],
        parts[2],
        parts[3],
        parts[4],
        grad_out.T.astype(F32),
    )


def solution(mesh):
    placed = (
        P("dp", "tensor", None),
        P("dp", "tensor", None),
        P(),
        P("dp", None, "tensor"),
        P("dp", None),
        P("dp", "tensor"),
        P(None, "tensor"),
        P("tensor"),
        P(),
        P(),
        P("tensor"),
        P("tensor"),
        P("tensor"),
        P("tensor"),
        P("tensor", "dp"),
    )
    return jax.shard_map(
        functools.partial(on_device, mesh.shape["dp"], mesh.shape["tensor"]),
        mesh=mesh,
        in_specs=placed,
        out_specs=(
            P("dp", "tensor", None),
            P("dp", "tensor", None),
            P(),
            P("dp", None, "tensor"),
            P("dp", None),
            P("dp", "tensor"),
            P(None, "tensor"),
            P("tensor"),
            P(),
            P(),
            P("tensor"),
            P("tensor"),
            P("tensor"),
            P("tensor"),
            P("tensor", "dp"),
        ),
        check_vma=False,
    )
```

```python
import functools

import jax
import jax.numpy as jnp
from jax import lax
from jax.experimental import pallas as pl
from jax.experimental.pallas import tpu as pltpu
from jax.sharding import PartitionSpec as P

NSTATE = 128
SPAN = 256
INNER = 1536
PAD = 128
EPSILON = 1e-05
F32 = jnp.float32
BF16 = jnp.bfloat16
VMEM_LIMIT = 60 * 1024 * 1024


def mm(left, right, left_dim=1, right_dim=0):
    return lax.dot_general(
        left, right, (((left_dim,), (right_dim,)), ((), ())), preferred_element_type=F32
    )


def exact_mm(left, right):
    return lax.dot_general(
        left, right, (((1,), (0,)), ((), ())), preferred_element_type=F32,
        precision=lax.Precision.HIGHEST,
    )


def sigmoid(v):
    return 1.0 / (1.0 + jnp.exp(-v))


def iotas(size):
    return (
        lax.broadcasted_iota(jnp.int32, (size, size), 0),
        lax.broadcasted_iota(jnp.int32, (size, size), 1),
    )


def by_pair(values, pair, first_lanes):
    left = values[:, 2 * pair : 2 * pair + 1]
    right = values[:, 2 * pair + 1 : 2 * pair + 2]
    return jnp.where(first_lanes, left, right)


def steps_of(step_raw, hp):
    shifted = step_raw + hp[0:1, :]
    step = jnp.maximum(shifted, 0.0) + jnp.log1p(jnp.exp(-jnp.abs(shifted)))
    return shifted, step, -jnp.exp(hp[1:2, :]) * step


def forward_kernel(
    normed_ref, wcat_ref, cw_ref, hp_ref, ch_ref,
    raw_ref, conv_ref, scanned_ref, gated_ref, state_out_ref,
    buf, state, fresh_in,
):
    at = pl.program_id(0)
    span = normed_ref.shape[0]
    width = scanned_ref.shape[1]
    both = width + 2 * NSTATE

    @pl.when(at == 0)
    def _():
        buf[0:8, :] = jnp.zeros((8, both), F32)
        state[...] = jnp.zeros_like(state)

    @pl.when(at > 0)
    def _():
        buf[0:8, :] = buf[span : span + 8, :]

    raw_ref[...] = mm(normed_ref[...], wcat_ref[...])
    buf[8 : 8 + span, :] = raw_ref[:, width : width + both]
    conv = cw_ref[4:5, :] + cw_ref[0:1, :] * buf[5 : 5 + span, :]
    for tap in range(1, 4):
        conv = conv + cw_ref[tap : tap + 1, :] * buf[5 + tap : 5 + tap + span, :]
    conv_ref[...] = conv
    act = (conv * sigmoid(conv)).astype(BF16)
    km = act[:, width : width + NSTATE]
    qm = act[:, width + NSTATE :]
    shifted, step, rate = steps_of(raw_ref[:, width + both :], hp_ref[...])
    rows, cols = iotas(span)
    causal = cols <= rows
    cum = exact_mm(jnp.where(causal, 1.0, 0.0), rate)
    cum_t = cum.T
    grow = jnp.exp(cum)
    last = cum[span - 1 : span, :]
    tail = jnp.exp(last - cum)
    total = jnp.exp(last)
    scores = jnp.where(causal, mm(qm, km, 1, 1), 0.0)
    state_now = state[...]
    state_out_ref[...] = state_now
    inter = mm(qm, state_now.astype(BF16))
    first = lax.broadcasted_iota(jnp.int32, (span, 128), 1) < 64
    for pair in range(width // 128):
        lanes = slice(pair * 128, pair * 128 + 128)
        x = act[:, lanes].astype(F32)
        u = x * by_pair(step, pair, first)
        fresh_in[:, lanes] = (u * by_pair(tail, pair, first)).astype(BF16)
        low_u = u.astype(BF16)
        ys = []
        for head in (2 * pair, 2 * pair + 1):
            gap = jnp.minimum(cum[:, head : head + 1] - cum_t[head : head + 1, :], 0.0)
            ys.append(mm((jnp.exp(gap) * scores).astype(BF16), low_u))
        y = jnp.where(first, ys[0], ys[1]) + inter[:, lanes] * by_pair(grow, pair, first)
        scanned_ref[:, lanes] = y + ch_ref[0:1, lanes] * x
    fresh = mm(km, fresh_in[...], 0, 0)
    for pair in range(width // 128):
        lanes = slice(pair * 128, pair * 128 + 128)
        state[:, lanes] = (
            by_pair(total, pair, first[0:1]) * state_now[:, lanes] + fresh[:, lanes]
        )
    gate_z = raw_ref[:, 0:width]
    gated = scanned_ref[...] * (gate_z * sigmoid(gate_z))
    gated_ref[...] = gated


def backward_kernel(
    normed_ref, raw_ref, conv_ref, scanned_ref, state_ref, dng_ref, stats_ref,
    wcat_ref, cw_ref, hp_ref, ch_ref, sum_ref,
    partial_ref, grads_a_ref, grads_b_ref, gcw_ref, ghp_ref, gch_ref,
    adjoint, buf, acc, dye, ut, dz, prod, score_sum,
):
    at = pl.program_id(0)
    span = normed_ref.shape[0]
    width = scanned_ref.shape[1]
    both = width + 2 * NSTATE

    @pl.when(at == 0)
    def _():
        buf[span : span + 8, :] = jnp.zeros((8, both), F32)
        adjoint[...] = jnp.zeros_like(adjoint)
        acc[...] = jnp.zeros_like(acc)
        gcw_ref[...] = jnp.zeros_like(gcw_ref)
        ghp_ref[...] = jnp.zeros_like(ghp_ref)
        gch_ref[...] = jnp.zeros_like(gch_ref)

    @pl.when(at > 0)
    def _():
        buf[span : span + 8, :] = buf[0:8, :]

    stats = jnp.concatenate([stats_ref[...], jnp.zeros((PAD - 8, span), F32)], axis=0).T
    scale = lax.rsqrt(stats[:, 0:1] / INNER + EPSILON)
    pull = scale * scale * scale * stats[:, 1:2] / INNER
    gate_z = raw_ref[:, 0:width]
    sig = sigmoid(gate_z)
    silu = gate_z * sig
    scanned = scanned_ref[...]
    gated = scanned * silu
    dng = dng_ref[...]
    d_gated = scale * (dng * ch_ref[1:2, :]) - gated * pull
    gch_ref[1:2, :] += jnp.sum(dng * gated * scale, axis=0, keepdims=True)
    dy = d_gated * silu
    dz[:, 0:width] = (d_gated * scanned * (sig * (1.0 + gate_z * (1.0 - sig)))).astype(BF16)

    conv = conv_ref[...]
    sig_conv = sigmoid(conv)
    act = (conv * sig_conv).astype(BF16)
    slope = sig_conv * (1.0 + conv * (1.0 - sig_conv))
    km = act[:, width : width + NSTATE]
    qm = act[:, width + NSTATE :]
    hp = hp_ref[...]
    shifted, step, rate = steps_of(raw_ref[:, width + both :], hp)
    rows, cols = iotas(span)
    causal = cols <= rows
    cum = exact_mm(jnp.where(causal, 1.0, 0.0), rate)
    cum_t = cum.T
    grow = jnp.exp(cum)
    last = cum[span - 1 : span, :]
    tail = jnp.exp(last - cum)
    total = jnp.exp(last)
    scores = mm(qm, km, 1, 1)
    state = state_ref[...]
    low_state = state.astype(BF16)
    adj = adjoint[...]
    low_adj = adj.astype(BF16)
    inter = mm(qm, low_state)
    du_state = mm(km, low_adj)
    first = lax.broadcasted_iota(jnp.int32, (span, 128), 1) < 64
    lane = lax.broadcasted_iota(jnp.int32, (span, PAD), 1)
    row_sums = jnp.zeros((span, PAD), F32)
    col_sums = []
    for pair in range(width // 128):
        lanes = slice(pair * 128, pair * 128 + 128)
        x = act[:, lanes].astype(F32)
        step_pair = by_pair(step, pair, first)
        tail_pair = by_pair(tail, pair, first)
        u = x * step_pair
        low_u = u.astype(BF16)
        u_tail = u * tail_pair
        ut[:, lanes] = u_tail.astype(BF16)
        dy_pair = dy[:, lanes]
        low_dy = dy_pair.astype(BF16)
        dy_grow = dy_pair * by_pair(grow, pair, first)
        dye[:, lanes] = dy_grow.astype(BF16)
        prod[0:span, lanes] = dy_grow * inter[:, lanes]
        prod[span : 2 * span, lanes] = u_tail * du_state[:, lanes]
        dus = []
        for head in (2 * pair, 2 * pair + 1):
            mine = first if head % 2 == 0 else jnp.logical_not(first)
            d_weights = mm(jnp.where(mine, low_dy, jnp.zeros_like(low_dy)), low_u, 1, 1)
            gap = cum[:, head : head + 1] - cum_t[head : head + 1, :]
            table = jnp.exp(jnp.where(causal, gap, -1e30))
            weights = table * scores
            d_scores = table * d_weights
            if head == 0:
                score_sum[...] = d_scores
            else:
                score_sum[...] += d_scores
            moved = weights * d_weights
            row_sums = jnp.where(
                lane == head, jnp.sum(moved, axis=1, keepdims=True), row_sums
            )
            col_sums.append(jnp.sum(moved, axis=0, keepdims=True))
            dus.append(mm(weights.astype(BF16), low_dy, 0, 0))
        du = jnp.where(first, dus[0], dus[1]) + du_state[:, lanes] * tail_pair
        prod[2 * span : 3 * span, lanes] = x * du
        gch_ref[0:1, lanes] += jnp.sum(dy_pair * x, axis=0, keepdims=True)
        dx = step_pair * du + ch_ref[0:1, lanes] * dy_pair
        buf[0:span, lanes] = dx * slope[:, lanes]
    col_sums.append(jnp.zeros((PAD - len(col_sums), span), F32))
    col_sums = jnp.concatenate(col_sums, axis=0).T
    prods = prod[...]
    high = prods.astype(BF16)
    low = (prods - high.astype(F32)).astype(BF16)
    summer = sum_ref[...]
    heads = mm(high, summer) + mm(low, summer)
    met = jnp.sum(adj * state, axis=0, keepdims=True)
    met = jnp.broadcast_to(met, (8, width))
    met_high = met.astype(BF16)
    met_low = (met - met_high.astype(F32)).astype(BF16)
    met = (mm(met_high, summer) + mm(met_low, summer))[0:1, :]
    d_rate = (
        exact_mm(jnp.where(cols >= rows, 1.0, 0.0), row_sums - col_sums + heads[0:span])
        + exact_mm(jnp.where(cols < rows, 1.0, 0.0), heads[span : 2 * span])
        + total * met
    )
    d_step = heads[2 * span :] - jnp.exp(hp[1:2, :]) * d_rate
    d_step_raw = d_step * sigmoid(shifted)
    ghp_ref[0:1, :] += jnp.sum(d_step_raw, axis=0, keepdims=True)
    ghp_ref[1:2, :] += jnp.sum(d_rate * rate, axis=0, keepdims=True)
    dz[:, width + both :] = d_step_raw.astype(BF16)

    low_sum = score_sum[...].astype(BF16)
    dk = mm(low_sum, qm, 0, 0) + mm(ut[...], low_adj, 1, 1)
    dq = mm(low_sum, km) + mm(dye[...], low_state, 1, 1)
    buf[0:span, width : width + NSTATE] = dk * slope[:, width : width + NSTATE]
    buf[0:span, width + NSTATE : both] = dq * slope[:, width + NSTATE :]
    raw = raw_ref[:, width : width + both]
    gcw_ref[4:5, :] += jnp.sum(buf[0:span, :], axis=0, keepdims=True)
    d_raw = jnp.zeros((span, both), F32)
    for tap in range(4):
        moved = buf[3 - tap : 3 - tap + span, :]
        d_raw = d_raw + cw_ref[tap : tap + 1, :] * moved
        gcw_ref[tap : tap + 1, :] += jnp.sum(raw * moved, axis=0, keepdims=True)
    dz[:, width : width + both] = d_raw.astype(BF16)

    low_dz = dz[...]
    partial_ref[...] = mm(low_dz, wcat_ref[...], 1, 1).astype(BF16)
    acc[...] += mm(normed_ref[...], low_dz, 0, 0)
    fresh = mm(qm, dye[...], 0, 0)
    for pair in range(width // 128):
        lanes = slice(pair * 128, pair * 128 + 128)
        adjoint[:, lanes] = by_pair(total, pair, first[0:1]) * adj[:, lanes] + fresh[:, lanes]

    @pl.when(at == pl.num_programs(0) - 1)
    def _():
        cut = grads_a_ref.shape[1]
        grads_a_ref[...] = acc[:, :cut].astype(BF16)
        grads_b_ref[...] = acc[:, cut:].astype(BF16)


def forward_part(normed, wcat, cw, hp, ch):
    length, model = normed.shape
    width = ch.shape[1]
    both = width + 2 * NSTATE
    cat = wcat.shape[1]
    blocks = length // SPAN
    row = lambda cols: pl.BlockSpec((SPAN, cols), lambda i: (i, 0))
    whole = lambda arr: pl.BlockSpec(arr.shape, lambda i: (0, 0))
    shape = lambda r, c: jax.ShapeDtypeStruct((r, c), F32)
    return pl.pallas_call(
        forward_kernel,
        grid=(blocks,),
        in_specs=[row(model), whole(wcat), whole(cw), whole(hp), whole(ch)],
        out_specs=[
            row(cat), row(both), row(width), row(width),
            pl.BlockSpec((NSTATE, width), lambda i: (i, 0)),
        ],
        out_shape=[
            shape(length, cat), shape(length, both), shape(length, width), shape(length, width),
            shape(blocks * NSTATE, width),
        ],
        scratch_shapes=[
            pltpu.VMEM((SPAN + 8, both), F32),
            pltpu.VMEM((NSTATE, width), F32),
            pltpu.VMEM((SPAN, width), BF16),
        ],
        compiler_params=pltpu.CompilerParams(vmem_limit_bytes=VMEM_LIMIT),
        cost_estimate=pl.CostEstimate(
            flops=2 * length * (model * (cat + width) + 4 * SPAN * width),
            bytes_accessed=25 * 2**20, transcendentals=length * width * 6,
        ),
        name="mixer_forward",
    )(normed, wcat, cw, hp, ch)


def backward_part(normed, raw, conv, scanned, states, dng, stats, wcat, cw, hp, ch):
    length, model = normed.shape
    width = ch.shape[1]
    both = width + 2 * NSTATE
    cat = wcat.shape[1]
    blocks = length // SPAN
    cut = cat // 256 * 128
    summer = (
        lax.broadcasted_iota(jnp.int32, (width, PAD), 0) // 64
        == lax.broadcasted_iota(jnp.int32, (width, PAD), 1)
    ).astype(BF16)
    row = lambda cols: pl.BlockSpec((SPAN, cols), lambda i: (blocks - 1 - i, 0))
    whole = lambda arr: pl.BlockSpec(arr.shape, lambda i: (0, 0))
    return pl.pallas_call(
        backward_kernel,
        grid=(blocks,),
        in_specs=[
            row(model), row(cat), row(both), row(width),
            pl.BlockSpec((NSTATE, width), lambda i: (blocks - 1 - i, 0)), row(width), pl.BlockSpec((8, SPAN), lambda i: (0, blocks - 1 - i)),
            whole(wcat), whole(cw), whole(hp), whole(ch), whole(summer),
        ],
        out_specs=[
            row(model), pl.BlockSpec((model, cut), lambda i: (0, 0)),
            pl.BlockSpec((model, cat - cut), lambda i: (0, 0)), whole(cw), whole(hp), whole(ch)],
        out_shape=[
            jax.ShapeDtypeStruct((length, model), BF16),
            jax.ShapeDtypeStruct((model, cut), BF16),
            jax.ShapeDtypeStruct((model, cat - cut), BF16),
            jax.ShapeDtypeStruct(cw.shape, F32),
            jax.ShapeDtypeStruct(hp.shape, F32),
            jax.ShapeDtypeStruct(ch.shape, F32),
        ],
        scratch_shapes=[
            pltpu.VMEM((NSTATE, width), F32),
            pltpu.VMEM((SPAN + 8, both), F32),
            pltpu.VMEM((model, cat), F32),
            pltpu.VMEM((SPAN, width), BF16),
            pltpu.VMEM((SPAN, width), BF16),
            pltpu.VMEM((SPAN, cat), BF16),
            pltpu.VMEM((3 * SPAN, width), F32),
            pltpu.VMEM((SPAN, SPAN), F32),
        ],
        compiler_params=pltpu.CompilerParams(vmem_limit_bytes=VMEM_LIMIT),
        cost_estimate=pl.CostEstimate(
            flops=2 * length * (2 * model * cat + 10 * SPAN * width),
            bytes_accessed=25 * 2**20, transcendentals=length * width * 8,
        ),
        name="mixer_adjoint",
    )(normed, raw, conv, scanned, states, dng, stats, wcat, cw, hp, ch, summer)


def swap(values, bit, axis, size):
    return lax.ppermute(values, axis, [(i, i ^ bit) for i in range(size)])


def scatter_steps(held, size, order, start, stop):
    me = lax.axis_index("dp")
    left = [bit for bit in range(size.bit_length() - 2, -1, -1) if bit not in order[:start]]
    for bit in order[start:stop]:
        axis = left.index(bit)
        mine = (me >> bit) & 1
        keep = lax.dynamic_index_in_dim(held, mine, axis, keepdims=False)
        send = lax.dynamic_index_in_dim(held, 1 - mine, axis, keepdims=False)
        got = swap(send, 1 << bit, "dp", size)
        held = (keep.astype(F32) + got.astype(F32)).astype(BF16)
        left.pop(axis)
    return held


def scatter_sum(values, size, order, stop=None):
    rows = values.shape[0] // size
    held = values.reshape((2,) * len(order) + (rows, values.shape[1]))
    return scatter_steps(held, size, order, 0, stop)


def scatter_rest(held, size, order, start):
    return scatter_steps(held, size, order, start, None)


def whole_sum(values, axis, size):
    bit = 1
    while bit < size:
        values = values + swap(values, bit, axis, size)
        bit *= 2
    return values


def token_scatter(values, size):
    if size != 2:
        return lax.psum_scatter(values, "tensor", scatter_dimension=0, tiled=True).astype(F32)
    me = lax.axis_index("tensor")
    half = values.shape[0] // 2
    keep = lax.dynamic_slice_in_dim(values, me * half, half, 0)
    send = lax.dynamic_slice_in_dim(values, (1 - me) * half, half, 0)
    return keep.astype(F32) + swap(send, 1, "tensor", 2).astype(F32)


def token_gather(values, size):
    if size != 2:
        return lax.all_gather(values, "tensor", axis=0, tiled=True)
    got = swap(values, 1, "tensor", 2)
    is_first = lax.axis_index("tensor") == 0
    return jnp.concatenate(
        [jnp.where(is_first, values, got), jnp.where(is_first, got, values)], axis=0
    )


def on_device(
    dp, tp,
    tokens, cotangent, norm_in, gate_inner_projection, proj_bc, proj_dt, conv_inner,
    bias_inner, conv_bc, bias_bc, step_bias, log_decay, skip_gain, norm_gate, proj_out,
):
    width = gate_inner_projection.shape[2]
    heads = step_bias.shape[0]
    model = tokens.shape[2]
    share = model // dp
    cat = 2 * width + 2 * NSTATE + PAD
    packed = jnp.concatenate(
        [
            gate_inner_projection.reshape(share, 2 * width),
            proj_bc,
            jnp.pad(proj_dt, ((0, 0), (0, PAD - heads))),
        ],
        axis=1,
    )
    wcat = lax.all_gather(packed, "dp", axis=0, tiled=True)
    token_rows = tokens[0].astype(F32)
    inv_rms = lax.rsqrt(jnp.mean(token_rows * token_rows, axis=-1, keepdims=True) + EPSILON)
    local_normed = (token_rows * inv_rms * norm_in).astype(BF16)
    normed = token_gather(local_normed, tp)
    cot = token_gather(cotangent[0], tp)
    out_rows, wcat, normed = lax.optimization_barrier((proj_out.T, wcat, normed))
    out_t = lax.all_gather(out_rows, "dp", axis=0, tiled=True)
    cw = jnp.pad(
        jnp.concatenate(
            [
                jnp.concatenate([conv_inner, conv_bc], axis=1),
                jnp.concatenate([bias_inner, bias_bc])[None],
            ],
            axis=0,
        ),
        ((0, 3), (0, 0)),
    )
    hp = jnp.pad(jnp.stack([step_bias, log_decay]), ((0, 6), (0, PAD - heads)))
    ch = jnp.pad(jnp.stack([jnp.repeat(skip_gain, width // heads), norm_gate]), ((0, 6), (0, 0)))
    raw, conv, scanned, gated, states = forward_part(normed, wcat, cw, hp, ch)
    dng = mm(cot, out_t)
    stats = jnp.stack(
        [jnp.sum(gated * gated, axis=1), jnp.sum(dng * norm_gate * gated, axis=1)]
    )
    stats = jnp.pad(stats, ((0, 6), (0, 0)))
    stats = whole_sum(stats, "tensor", tp)
    scale = lax.rsqrt(stats[0][:, None] / INNER + EPSILON)
    gate_normed = (gated * scale * norm_gate).astype(BF16)
    branch_part = mm(gate_normed, out_t, 1, 1).astype(BF16)
    bits = dp.bit_length() - 1
    order = tuple(range(bits))
    other = (0,) + tuple(range(2, bits)) + (1,)
    out_part = mm(cot, gate_normed, 0, 0).astype(BF16)
    branch_part, out_part, stats = lax.optimization_barrier((branch_part, out_part, stats))
    branch = token_scatter(branch_part, tp)
    out_first = (1,) + tuple(b for b in order if b != 1)
    grad_out = scatter_sum(out_part, dp, out_first, 1)
    partial, grads_a, grads_b, gcw, ghp, gch = backward_part(
        normed, raw, conv, scanned, states, dng, stats, wcat, cw, hp, ch
    )
    branch, grad_out, partial, grads_a, grads_b = lax.optimization_barrier(
        (branch, grad_out, partial, grads_a, grads_b)
    )
    block_out = (token_rows + branch).astype(BF16)[None]
    grad_out = scatter_rest(grad_out, dp, out_first, 1)
    grads = jnp.concatenate(
        [scatter_sum(grads_a, dp, order), scatter_sum(grads_b, dp, other)], axis=1
    )
    d_rows = token_scatter(partial, tp)
    gained = norm_in * d_rows
    dotted = jnp.sum(token_rows * gained, axis=-1, keepdims=True)
    input_grad = (
        cotangent[0].astype(F32)
        + inv_rms * gained
        - token_rows * (inv_rms * inv_rms * inv_rms * dotted / model)
    )[None]
    grad_norm_in = jnp.sum(d_rows * token_rows * inv_rms, axis=0)
    grad_skip = jnp.sum(gch[0].reshape(heads, -1), axis=1)
    mine = [gcw[:5, :width].reshape(-1), ghp[0, :heads], ghp[1, :heads], grad_skip, gch[1]]
    common = [gcw[:5, width:].reshape(-1), grad_norm_in]
    sizes = [v.shape[0] for v in mine + common]
    flat = jnp.concatenate(mine + common)
    count = flat.shape[0]
    flat = jnp.pad(flat, (0, -count % 1024)).reshape(-1, 128)
    flat = whole_sum(flat, "dp", dp).reshape(-1)[:count]
    own = sum(sizes[: len(mine)])
    grad_bc = grads[:, 2 * width : 2 * width + 2 * NSTATE].astype(F32)
    shared = jnp.concatenate([grad_bc.reshape(-1), flat[own:]])
    shared = whole_sum(shared.reshape(-1, 128), "tensor", tp).reshape(-1)
    grad_bc = shared[: grad_bc.size].reshape(grad_bc.shape)
    shared = shared[grad_bc.size :]
    parts = jnp.split(flat[:own], [sum(sizes[:i]) for i in range(1, len(mine))])
    gconv = parts[0].reshape(5, width)
    gbc = shared[: sizes[len(mine)]].reshape(5, 2 * NSTATE)
    return (
        block_out,
        input_grad,
        shared[sizes[len(mine)] :],
        grads[:, : 2 * width].astype(F32).reshape(share, 2, width),
        grad_bc,
        grads[:, 2 * width + 2 * NSTATE :][:, :heads].astype(F32),
        gconv[:4],
        gconv[4],
        gbc[:4],
        gbc[4],
        parts[1],
        parts[2],
        parts[3],
        parts[4],
        grad_out.T.astype(F32),
    )


def solution(mesh):
    placed = (
        P("dp", "tensor", None),
        P("dp", "tensor", None),
        P(),
        P("dp", None, "tensor"),
        P("dp", None),
        P("dp", "tensor"),
        P(None, "tensor"),
        P("tensor"),
        P(),
        P(),
        P("tensor"),
        P("tensor"),
        P("tensor"),
        P("tensor"),
        P("tensor", "dp"),
    )
    return jax.shard_map(
        functools.partial(on_device, mesh.shape["dp"], mesh.shape["tensor"]),
        mesh=mesh,
        in_specs=placed,
        out_specs=(
            P("dp", "tensor", None),
            P("dp", "tensor", None),
            P(),
            P("dp", None, "tensor"),
            P("dp", None),
            P("dp", "tensor"),
            P(None, "tensor"),
            P("tensor"),
            P(),
            P(),
            P("tensor"),
            P("tensor"),
            P("tensor"),
            P("tensor"),
            P("tensor", "dp"),
        ),
        check_vma=False,
    )
```
